256 devices in a mesh: row: 32 (over x, z_hi, core), col: 8 (over y, z_lo).
Axes of the slice: x: 4, y: 4, z: 8 (z_hi: 4, z_lo: 2; z = z_hi * 2 + z_lo), core: 2. Of those that a mesh axis runs over, the one named last changes fastest.
Arguments:
- image: bfloat16 [1536, 2048, 256], P('row', 'col'), may hold values from -6 to 6
- proj_in: bfloat16 [256, 512], replicated, may hold values from -0.375 to 0.375
- taps_wide: float32 [3, 512], replicated, may hold values from -3 to 3
- taps_tall: float32 [3, 512], replicated, may hold values from -3 to 3
- proj_out: bfloat16 [512, 256], replicated, may hold values from -0.25 to 0.25
- bias: float32 [256], replicated, may hold values from -3 to 3
Outputs:
- result: bfloat16 [1536, 2048, 256], P('row', 'col')
The draws below stay inside these ranges and needn't reach their ends.
All inputs are finite; a program needn't handle non-finite values.
Results may differ from the reference program's by a relative error of at most 0.0054.
Values may be sent and summed in bfloat16 or wider, within the bound.
A program may use at most 192 MiB of HBM per device.

```python
import jax
import jax.numpy as jnp
from jax import lax

C = 256
R = 512
TH = 48
H = 1536
W = 2048
N_ROW = 32


def shard_levels(stream_key, dims, cuts, smallest, largest):
    gain = 1.0
    for axis_at, parts in cuts:
        heights = jax.random.uniform(jax.random.fold_in(jax.random.fold_in(stream_key, 6), axis_at), (parts,), jnp.float32, smallest / len(cuts), largest / len(cuts))
        gain = gain * jnp.repeat(jnp.exp(heights), dims[axis_at] // parts).reshape((-1,) + (1,) * (len(dims) - 1 - axis_at))
    return gain


def bell_draw(key, extent, width, bound, cuts=(), kind=jnp.bfloat16):
    entries = jax.random.normal(key, extent, jnp.float32) * width
    if len(cuts) > 0:
        entries = shard_levels(key, extent, cuts, -0.22, 0.18) * entries
    return jnp.clip(entries, min=-bound, max=bound).astype(kind)


def setup_inputs(seed: int = 0) -> dict:
    splits = jax.random.split(jax.random.key(seed), 7)
    image = bell_draw(splits[0], (H, W, C), 1.0, 6.0, ((0, 32), (1, 8)))
    proj_in = bell_draw(splits[1], (C, R), C ** -0.5, 0.375)
    taps_wide = bell_draw(splits[2], (3, R), 0.6, 3.0, (), jnp.float32)
    taps_tall = bell_draw(splits[3], (3, R), 0.6, 3.0, (), jnp.float32)
    proj_out = bell_draw(splits[4], (R, C), R ** -0.5, 0.25)
    bias = bell_draw(splits[5], (C,), 0.5, 3.0, (), jnp.float32)
    return {"image": image, "proj_in": proj_in, "taps_wide": taps_wide, "taps_tall": taps_tall, "proj_out": proj_out, "bias": bias}


def reference(image, proj_in, taps_wide, taps_tall, proj_out, bias):
    zero_row = jnp.zeros((1, W, C), jnp.bfloat16)
    padded_image = jnp.concatenate([zero_row, image, zero_row], axis=0)
    weight_in = proj_in.astype(jnp.float32)
    weight_out = proj_out.astype(jnp.float32)

    def one_block(index):
        rows = lax.dynamic_slice_in_dim(padded_image, (index * TH).astype(jnp.int32), TH + 2, 0)
        lifted = jnp.einsum("hwc,cr->hrw", rows.astype(jnp.float32), weight_in).astype(jnp.bfloat16)
        side = jnp.pad(lifted, ((0, 0), (0, 0), (1, 1)))
        widened = (taps_wide[0][:, None] * side[:, :, :-2] + taps_wide[1][:, None] * side[:, :, 1:-1]
                   + taps_wide[2][:, None] * side[:, :, 2:]).astype(jnp.bfloat16)
        heightened = (taps_tall[0][:, None] * widened[:-2] + taps_tall[1][:, None] * widened[1:-1]
                      + taps_tall[2][:, None] * widened[2:]).astype(jnp.bfloat16)
        mixed = jnp.einsum("hrw,rc->hwc", heightened.astype(jnp.float32), weight_out) + bias
        centre = rows[1:-1].astype(jnp.float32)
        return (centre + jax.nn.silu(mixed)).astype(jnp.bfloat16)

    blocks = lax.map(one_block, jnp.arange(N_ROW, dtype=jnp.int32))
    return blocks.reshape(H, W, C)
```

```python
import functools

import jax
import jax.numpy as jnp
from jax import lax
from jax.experimental import pallas as pl
from jax.experimental.pallas import tpu as pltpu
from jax.sharding import PartitionSpec as P

MESH = pl.DeviceIdType.MESH
F32, BF16 = jnp.float32, jnp.bfloat16
EDGE = 16
STAGES = 3
PAIRS = 3


def spread_kernel(
    rows, cols,
    image, proj_in, taps_wide, taps_tall, proj_out,
    centre, left, right, weights,
    strip_l, strip_r, edge_l, edge_r, halo_l, halo_r, corners, halo_lf, halo_rf, p_in, t_wide, t_tall, p_out,
    local_sem, stage_sem, send_sem, recv_sem,
):
    th, tw, c = image.shape
    r, k = lax.axis_index("row"), lax.axis_index("col")
    up, down = lax.rem(r + rows - 1, rows), lax.rem(r + 1, rows)
    west, east = lax.rem(k + cols - 1, cols), lax.rem(k + 1, cols)
    around = [(up, k), (down, k), (r, west), (r, east), (up, west), (up, east), (down, west), (down, east)]

    barrier = pltpu.get_barrier_semaphore()
    for to in around:
        pl.semaphore_signal(barrier, inc=1, device_id=to, device_id_type=MESH)

    local = [
        pltpu.make_async_copy(src, dst, local_sem.at[i])
        for i, (src, dst) in enumerate([
            (image.at[:, pl.ds(0, EDGE)], strip_l),
            (image.at[:, pl.ds(tw - EDGE, EDGE)], strip_r),
            (proj_in, p_in), (taps_wide, t_wide), (taps_tall, t_tall), (proj_out, p_out),
        ])
    ]
    for copy in local:
        copy.start()
    step = th // STAGES

    def stage(s):
        return pltpu.make_async_copy(image.at[pl.ds(s * step, step)], centre.at[pl.ds(1 + s * step, step)], stage_sem.at[s])

    for s in range(STAGES):
        stage(s).start()

    pl.semaphore_wait(barrier, len(around))

    def send(i, src, dst, to):
        copy = pltpu.make_async_remote_copy(
            src_ref=src, dst_ref=dst, send_sem=send_sem.at[i], recv_sem=recv_sem.at[i], device_id=to, device_id_type=MESH
        )
        copy.start()
        return copy

    row_copies = [
        send(0, image.at[0], centre.at[th + 1], (up, k)),
        send(1, image.at[th - 1], centre.at[0], (down, k)),
    ]
    local[0].wait()
    local[1].wait()
    edge_l[...] = strip_l[:, 0, :]
    edge_r[...] = strip_r[:, EDGE - 1, :]
    top, bottom = pl.ds(0, EDGE), pl.ds(th - EDGE, EDGE)
    edge_copies = [
        send(2, edge_l, halo_r, (r, west)),
        send(3, edge_r, halo_l, (r, east)),
        send(4, edge_l.at[top], corners.at[0], (up, west)),
        send(5, edge_r.at[top], corners.at[1], (up, east)),
        send(6, edge_l.at[bottom], corners.at[2], (down, west)),
        send(7, edge_r.at[bottom], corners.at[3], (down, east)),
    ]
    for copy in local[2:]:
        copy.wait()

    def shift(h, before, after):
        v = centre[h]
        p = jnp.concatenate([v[1:], after], 0)
        right[h] = p
        left[h] = jnp.concatenate([before, v[:1], p[:-2]], 0)

    zero = jnp.zeros((1, c), BF16)

    def taps(j, carry):
        stage(j).wait()
        wide = t_wide[pl.ds(j, 1)]
        base = p_in[...].astype(F32)
        g = []
        for i in range(3):
            a = base * (wide * t_tall[pl.ds(i, 1)])
            high = a.astype(BF16)
            low = (a - high.astype(F32)).astype(BF16)
            g.append(
                jnp.dot(high, p_out[...], preferred_element_type=F32) + jnp.dot(low, p_out[...], preferred_element_type=F32)
            )
        at = pl.ds(pl.multiple_of(j * c, c), c)
        ends = 0.25 * (g[0] + g[2])
        middle = 0.25 * g[1]
        weights[0, at] = (0.5 * g[0]).astype(BF16)
        weights[1, at] = (ends + middle).astype(BF16)
        weights[2, at] = (ends - middle).astype(BF16)
        weights[3, at] = (0.5 * g[2]).astype(BF16)
        for h in range(step):
            shift(1 + j * step + h, zero, zero)
        return carry

    lax.fori_loop(0, STAGES, taps, 0)

    for copy in edge_copies:
        copy.wait()
    halo_lf[...] = jnp.where(k > 0, halo_l[...].astype(F32), 0.0)
    halo_rf[...] = jnp.where(k < cols - 1, halo_r[...].astype(F32), 0.0)
    line = lax.broadcasted_iota(jnp.int32, (EDGE, c), 0)

    def mend(h, carry):
        tile = left[h + 1, pl.ds(0, EDGE)].astype(F32)
        left[h + 1, pl.ds(0, EDGE)] = jnp.where(line == 0, halo_lf[pl.ds(h, 1)], tile).astype(BF16)
        tile = right[h + 1, pl.ds(tw - EDGE, EDGE)].astype(F32)
        right[h + 1, pl.ds(tw - EDGE, EDGE)] = jnp.where(line == EDGE - 1, halo_rf[pl.ds(h, 1)], tile).astype(BF16)
        return carry

    lax.fori_loop(0, th, mend, 0)

    for copy in row_copies:
        copy.wait()

    def corner(i, at, edge):
        return jnp.where(edge, 0.0, corners[i].astype(F32))[at : at + 1].astype(BF16)

    @pl.when(r == 0)
    def _():
        centre[0] = jnp.zeros((tw, c), BF16)

    @pl.when(r == rows - 1)
    def _():
        centre[th + 1] = jnp.zeros((tw, c), BF16)

    shift(0, corner(3, EDGE - 1, (k == 0) | (r == 0)), corner(2, EDGE - 1, (k == cols - 1) | (r == 0)))
    shift(th + 1, corner(1, 0, (k == 0) | (r == rows - 1)), corner(0, 0, (k == cols - 1) | (r == rows - 1)))


def spread(rows, cols, image, proj_in, taps_wide, taps_tall, proj_out):
    th, tw, c = image.shape
    rank = proj_in.shape[1]
    vmem, hbm = pl.BlockSpec(memory_space=pltpu.VMEM), pl.BlockSpec(memory_space=pltpu.HBM)
    tile = jax.ShapeDtypeStruct((th + 2, tw, c), BF16)
    return pl.pallas_call(
        functools.partial(spread_kernel, rows, cols),
        out_shape=(tile, tile, tile, jax.ShapeDtypeStruct((4, 3 * c, c), BF16)),
        in_specs=[hbm] * 5,
        out_specs=(vmem,) * 4,
        scratch_shapes=[
            pltpu.VMEM((th, EDGE, c), BF16),
            pltpu.VMEM((th, EDGE, c), BF16),
            pltpu.VMEM((th, c), BF16),
            pltpu.VMEM((th, c), BF16),
            pltpu.VMEM((th, c), BF16),
            pltpu.VMEM((th, c), BF16),
            pltpu.VMEM((4, EDGE, c), BF16),
            pltpu.VMEM((th, c), F32),
            pltpu.VMEM((th, c), F32),
            pltpu.VMEM((c, rank), BF16),
            pltpu.VMEM((3, rank), F32),
            pltpu.VMEM((3, rank), F32),
            pltpu.VMEM((rank, c), BF16),
            pltpu.SemaphoreType.DMA((6,)),
            pltpu.SemaphoreType.DMA((STAGES,)),
            pltpu.SemaphoreType.DMA((8,)),
            pltpu.SemaphoreType.DMA((8,)),
        ],
        compiler_params=pltpu.CompilerParams(collective_id=0, has_side_effects=True, vmem_limit_bytes=32 * 2**20),
        cost_estimate=pl.CostEstimate(flops=18 * 2 * c * c * rank, bytes_accessed=8 * th * tw * c, transcendentals=0),
        name="spread",
    )(image, proj_in, taps_wide, taps_tall, proj_out)


def convolve_kernel(centre, left, right, weights, bias, out):
    chunk, tw, c = out.shape
    first = pl.program_id(0) * chunk
    half = 0.5 * bias[...]

    def moved(k):
        columns = []
        for ref in (left, centre, right):
            parts = []
            for q in range(PAIRS):
                d = [ref.at[first + 2 * q + i] for i in range(4)]
                if k == 0:
                    parts.append(d[0][...] - d[2][...])
                elif k == 1:
                    parts.append(d[1][...] + d[2][...])
                elif k == 2:
                    parts.append(d[2][...] - d[1][...])
                else:
                    parts.append(d[1][...] - d[3][...])
            columns.append(jnp.concatenate(parts, 0))
        return jnp.concatenate(columns, 1)

    def product(k):
        return jnp.dot(moved(k), weights[k], preferred_element_type=F32)

    def finish(y, i):
        t = y + half
        s = t + t * jnp.tanh(t)
        for q in range(PAIRS):
            o = centre[first + 2 * q + i + 1].astype(F32) + s[q * tw : (q + 1) * tw]
            out[2 * q + i] = o.astype(BF16)

    m1, m2 = product(1), product(2)
    total, difference = m1 + m2, m1 - m2
    finish(total + product(0), 0)
    finish(difference - product(3), 1)


def convolve(centre, left, right, weights, bias):
    th, tw, c = centre.shape
    th -= 2
    chunk = 2 * PAIRS
    vmem = pl.BlockSpec(memory_space=pltpu.VMEM)
    return pl.pallas_call(
        convolve_kernel,
        grid=(th // chunk,),
        out_shape=jax.ShapeDtypeStruct((th, tw, c), BF16),
        in_specs=[vmem] * 5,
        out_specs=pl.BlockSpec((chunk, tw, c), lambda i: (i, 0, 0)),
        compiler_params=pltpu.CompilerParams(vmem_limit_bytes=32 * 2**20),
        cost_estimate=pl.CostEstimate(flops=2 * 6 * th * tw * c * c, bytes_accessed=2 * th * tw * c, transcendentals=th * tw * c),
        name="convolve",
    )(centre, left, right, weights, bias)


def solution(mesh):
    rows, cols = mesh.shape["row"], mesh.shape["col"]

    def on_device(image, proj_in, taps_wide, taps_tall, proj_out, bias):
        tiles = spread(rows, cols, image, proj_in, taps_wide, taps_tall, proj_out)
        return convolve(*tiles, bias[None, :])

    in_specs = (P("row", "col", None), P(), P(), P(), P(), P())
    out_specs = P("row", "col", None)
    return jax.shard_map(on_device, mesh=mesh, in_specs=in_specs, out_specs=out_specs, check_vma=False)
```

```python
import functools

import jax
import jax.numpy as jnp
from jax import lax
from jax.experimental import pallas as pl
from jax.experimental.pallas import tpu as pltpu
from jax.sharding import PartitionSpec as P

MESH = pl.DeviceIdType.MESH
F32, BF16 = jnp.float32, jnp.bfloat16
EDGE = 16
PAIRS = 3
SPAN = 2 * PAIRS
DEEP = SPAN + 2


def products(pick, weights):
    def moved(k):
        columns = []
        for side in range(3):
            parts = []
            for q in range(PAIRS):
                a, b = ((0, 2), (1, 2), (2, 1), (1, 3))[k]
                a, b = pick(side, q, a), pick(side, q, b)
                parts.append(a + b if k == 1 else a - b)
            columns.append(jnp.concatenate(parts, 0))
        return jnp.concatenate(columns, 1)

    def product(k):
        return jnp.dot(moved(k), weights[k], preferred_element_type=F32)

    m1, m2 = product(1), product(2)
    total, difference = m1 + m2, m1 - m2
    return total + product(0), difference - product(3)


def activated(t):
    return t + t * jnp.tanh(t)


def get_rows(ref, at):
    return jnp.concatenate([ref[n, at] for n in range(ref.shape[0])], 1)


def put_rows(ref, at, value):
    wide = ref.shape[2]
    for n in range(ref.shape[0]):
        ref[n, at] = value[:, n * wide : (n + 1) * wide]


def shifted(v, before, after):
    p = jnp.concatenate([v[1:], after], 0)
    return jnp.concatenate([before, v[:1], p[:-2]], 0), p


def interior_kernel(
    rows, cols,
    image, proj_in, taps_wide, taps_tall, proj_out, bias,
    centre, done, last_l, last_r, weights,
    left_a, left_b, right_a, right_b, sum_a, sum_b,
    strip_l, strip_r, edge_l, edge_r, halo_l, halo_r, corners, column_l, column_r, before_l, before_r, fixed_l, fixed_r, own_l, own_r,
    p_in, t_wide, t_tall, p_out,
    local_sem, stage_sem, send_sem, recv_sem,
):
    th, tw, c = image.shape
    steps = th // SPAN - 1
    r, k = lax.axis_index("row"), lax.axis_index("col")
    up, down = lax.rem(r + rows - 1, rows), lax.rem(r + 1, rows)
    west, east = lax.rem(k + cols - 1, cols), lax.rem(k + 1, cols)
    around = [(up, k), (down, k), (r, west), (r, east), (up, west), (up, east), (down, west), (down, east)]

    barrier = pltpu.get_barrier_semaphore()
    for to in around:
        pl.semaphore_signal(barrier, inc=1, device_id=to, device_id_type=MESH)

    def stage(s):
        return pltpu.make_async_copy(image.at[pl.ds(s * SPAN, SPAN)], centre.at[pl.ds(1 + s * SPAN, SPAN)], stage_sem.at[s])

    stages = th // SPAN
    local = [
        pltpu.make_async_copy(src, dst, local_sem.at[i])
        for i, (src, dst) in enumerate([
            (proj_in, p_in), (taps_wide, t_wide), (taps_tall, t_tall), (proj_out, p_out),
            (image.at[:, pl.ds(0, EDGE)], strip_l),
            (image.at[:, pl.ds(tw - EDGE, EDGE)], strip_r),
        ])
    ]
    for copy in local[:4]:
        copy.start()
    for s in range(2):
        stage(s).start()
    for copy in local[4:]:
        copy.start()
    for s in range(2, stages):
        stage(s).start()

    zero = jnp.zeros((1, c), BF16)
    half = 0.5 * bias[...]

    def shift(at, left, right, i):
        left[i], right[i] = shifted(centre[at], zero, zero)

    for copy in local[:4]:
        copy.wait()
    for s in range(2):
        stage(s).wait()

    base = p_in[...].astype(F32)
    for j in range(3):
        wide = t_wide[pl.ds(j, 1)]
        g = []
        for i in range(3):
            a = base * (wide * t_tall[pl.ds(i, 1)])
            high = a.astype(BF16)
            low = (a - high.astype(F32)).astype(BF16)
            g.append(
                jnp.dot(high, p_out[...], preferred_element_type=F32) + jnp.dot(low, p_out[...], preferred_element_type=F32)
            )
        at = pl.ds(j * c, c)
        ends = 0.25 * (g[0] + g[2])
        middle = 0.25 * g[1]
        weights[0, at] = (0.5 * g[0]).astype(BF16)
        weights[1, at] = (ends + middle).astype(BF16)
        weights[2, at] = (ends - middle).astype(BF16)
        weights[3, at] = (0.5 * g[2]).astype(BF16)
        for i in range(j * DEEP // 3, (j + 1) * DEEP // 3):
            shift(2 + i, left_a, right_a, i)

    def multiply(s, left, right, total):
        first = 2 + SPAN * s

        def pick(side, q, i):
            if side == 1:
                return centre[first + 2 * q + i]
            return (left, None, right)[side][2 * q + i]

        total[0], total[1] = products(pick, weights)

    def finish(s, total):
        first = 2 + SPAN * s
        for i in range(2):
            t = total[i] + half
            y = activated(t)
            for q in range(PAIRS):
                row = first + 2 * q + i
                pair = pl.ds(1 + PAIRS * s + q, 1)
                done[row] = (centre[row + 1].astype(F32) + y[q * tw : (q + 1) * tw]).astype(BF16)
                before_l[i, pair] = t[q * tw : q * tw + 1]
                before_r[i, pair] = t[(q + 1) * tw - 1 : (q + 1) * tw]

    def prepare(s, left, right, old_left, old_right):
        for i in range(2):
            left[i] = old_left[SPAN + i]
            right[i] = old_right[SPAN + i]
        for i in range(2, DEEP):
            shift(jnp.minimum(2 + SPAN * s + i, th), left, right, i)

    stage(2).wait()
    multiply(0, left_a, right_a, sum_a)
    prepare(1, left_b, right_b, left_a, right_a)

    for copy in local[4:]:
        copy.wait()
    edge_l[...] = strip_l[:, 0, :]
    edge_r[...] = strip_r[:, EDGE - 1, :]
    for s in range(3, stages):
        stage(s).wait()

    pl.semaphore_wait(barrier, len(around))

    def send(i, src, dst, to):
        copy = pltpu.make_async_remote_copy(
            src_ref=src, dst_ref=dst, send_sem=send_sem.at[i], recv_sem=recv_sem.at[i], device_id=to, device_id_type=MESH
        )
        copy.start()
        return copy

    top, bottom = pl.ds(0, EDGE), pl.ds(th - EDGE, EDGE)
    row_copies = [
        send(0, image.at[0], centre.at[th + 1], (up, k)),
        send(1, image.at[th - 1], centre.at[0], (down, k)),
    ]
    edge_copies = [
        send(2, edge_l, halo_r, (r, west)),
        send(3, edge_r, halo_l, (r, east)),
        send(4, edge_l.at[top], corners.at[0], (up, west)),
        send(5, edge_r.at[top], corners.at[1], (up, east)),
        send(6, edge_l.at[bottom], corners.at[2], (down, west)),
        send(7, edge_r.at[bottom], corners.at[3], (down, east)),
    ]

    def two(n, carry):
        s = 2 * n + 1
        multiply(s, left_b, right_b, sum_b)
        finish(s - 1, sum_a)
        prepare(s + 1, left_a, right_a, left_b, right_b)
        multiply(s + 1, left_a, right_a, sum_a)
        finish(s, sum_b)
        prepare(s + 2, left_b, right_b, left_a, right_a)
        return carry

    lax.fori_loop(0, (steps - 1) // 2, two, 0)
    finish(steps - 1, sum_a)

    held = [*range(4), *range(th - SPAN + 2, th + 2)]
    for i, at in enumerate(held):
        if 0 < at <= th:
            shift(at, last_l, last_r, i)

    for copy in edge_copies:
        copy.wait()

    pairs = before_l.shape[1]
    fixed = []
    for side, (halo, column, edge, own, before, new, at, low, high) in enumerate([
        (halo_l, column_l, edge_l, own_l, before_l, fixed_l, 0, 3, 1),
        (halo_r, column_r, edge_r, own_r, before_r, fixed_r, 2 * c, 2, 0),
    ]):
        out_of_image = (k == 0) if side == 0 else (k == cols - 1)
        column[...] = jnp.zeros_like(column)
        put_rows(column, pl.ds(8, th), jnp.where(out_of_image, 0.0, halo[...].astype(F32)))
        upper = jnp.where(out_of_image | (r == 0), 0.0, corners[low].astype(F32))
        lower = jnp.where(out_of_image | (r == rows - 1), 0.0, corners[high].astype(F32))
        put_rows(column, pl.ds(7, 1), upper[EDGE - 1 :])
        put_rows(column, pl.ds(8 + th, 1), lower[:1])
        own[...] = jnp.zeros_like(own)
        put_rows(own, pl.ds(0, th), edge[...].astype(F32))
        d = [get_rows(column, pl.ds(7 + i, pairs, stride=2)) for i in range(4)]
        m = [
            jnp.dot(v.astype(BF16), weights[i, pl.ds(at, c)], preferred_element_type=F32)
            for i, v in enumerate([d[0] - d[2], d[1] + d[2], d[2] - d[1], d[1] - d[3]])
        ]
        for i, y in enumerate([m[0] + m[1] + m[2], m[1] - m[2] - m[3]]):
            lines = pl.ds(i, pairs, stride=2)
            put_rows(new, lines, get_rows(own, lines) + activated(before[i] + y))

    line = lax.broadcasted_iota(jnp.int32, (EDGE, c), 0)

    def placed(ref, h, start, where, value):
        tile = ref[h, pl.ds(start, EDGE)].astype(F32)
        ref[h, pl.ds(start, EDGE)] = jnp.where(line == where, value, tile).astype(BF16)

    def mend(h, carry):
        placed(done, h, 0, 0, get_rows(fixed_l, pl.ds(h, 1)))
        placed(done, h, tw - EDGE, EDGE - 1, get_rows(fixed_r, pl.ds(h, 1)))
        return carry

    lax.fori_loop(2, 2 + SPAN * steps, mend, 0)

    for copy in row_copies:
        copy.wait()

    @pl.when(r == 0)
    def _():
        centre[0] = jnp.zeros((tw, c), BF16)

    @pl.when(r == rows - 1)
    def _():
        centre[th + 1] = jnp.zeros((tw, c), BF16)

    for i, at in enumerate(held):
        if not 0 < at <= th:
            shift(at, last_l, last_r, i)
    for i, at in enumerate(held):
        placed(last_l, i, 0, 0, get_rows(column_l, pl.ds(7 + at, 1)))
        placed(last_r, i, tw - EDGE, EDGE - 1, get_rows(column_r, pl.ds(7 + at, 1)))


def interior(rows, cols, image, proj_in, taps_wide, taps_tall, proj_out, bias):
    th, tw, c = image.shape
    rank = proj_in.shape[1]
    pairs = -(-th // 32) * 16
    vmem, hbm = pl.BlockSpec(memory_space=pltpu.VMEM), pl.BlockSpec(memory_space=pltpu.HBM)
    return pl.pallas_call(
        functools.partial(interior_kernel, rows, cols),
        out_shape=(
            jax.ShapeDtypeStruct((th + 2, tw, c), BF16),
            jax.ShapeDtypeStruct((th, tw, c), BF16),
            jax.ShapeDtypeStruct((SPAN + 4, tw, c), BF16),
            jax.ShapeDtypeStruct((SPAN + 4, tw, c), BF16),
            jax.ShapeDtypeStruct((4, 3 * c, c), BF16),
        ),
        in_specs=[hbm] * 5 + [vmem],
        out_specs=(vmem,) * 5,
        scratch_shapes=[pltpu.VMEM((DEEP, tw, c), BF16)] * 4
        + [pltpu.VMEM((2, PAIRS * tw, c), F32)] * 2
        + [pltpu.VMEM((th, EDGE, c), BF16)] * 2
        + [pltpu.VMEM((th, c), BF16)] * 4
        + [pltpu.VMEM((4, EDGE, c), BF16)]
        + [pltpu.VMEM((c // 128, 2 * pairs + 16, 128), F32)] * 2
        + [pltpu.VMEM((2, pairs, c), F32)] * 2
        + [pltpu.VMEM((c // 128, 2 * pairs, 128), F32)] * 4
        + [
            pltpu.VMEM((c, rank), BF16),
            pltpu.VMEM((3, rank), F32),
            pltpu.VMEM((3, rank), F32),
            pltpu.VMEM((rank, c), BF16),
            pltpu.SemaphoreType.DMA((6,)),
            pltpu.SemaphoreType.DMA((th // SPAN,)),
            pltpu.SemaphoreType.DMA((8,)),
            pltpu.SemaphoreType.DMA((8,)),
        ],
        compiler_params=pltpu.CompilerParams(collective_id=0, has_side_effects=True, vmem_limit_bytes=36 * 2**20),
        cost_estimate=pl.CostEstimate(
            flops=2 * 6 * th * tw * c * c, bytes_accessed=2 * th * tw * c, transcendentals=th * tw * c
        ),
        name="interior",
    )(image, proj_in, taps_wide, taps_tall, proj_out, bias)


def border_kernel(centre, done, last_l, last_r, weights, bias, out, block, out_sem):
    th = done.shape[0]
    tw = done.shape[1]
    inner = pl.ds(2, th - SPAN)
    copies = [pltpu.make_async_copy(done.at[inner], out.at[inner], out_sem.at[0])]
    copies[0].start()
    half = 0.5 * bias[...]
    first = [0] + [th - SPAN + 2 * q for q in range(1, PAIRS)]

    def pick(side, q, i):
        if side == 1:
            return centre[first[q] + i]
        return (last_l, None, last_r)[side][(2 * q + 2 if q else 0) + i]

    for i, y in enumerate(products(pick, weights)):
        y = activated(y + half)
        for q in range(PAIRS):
            block[2 * q + i] = (centre[first[q] + i + 1].astype(F32) + y[q * tw : (q + 1) * tw]).astype(BF16)
    copies.append(pltpu.make_async_copy(block.at[pl.ds(0, 2)], out.at[pl.ds(0, 2)], out_sem.at[1]))
    copies.append(
        pltpu.make_async_copy(block.at[pl.ds(2, SPAN - 2)], out.at[pl.ds(th - SPAN + 2, SPAN - 2)], out_sem.at[2])
    )
    for copy in copies[1:]:
        copy.start()
    for copy in copies:
        copy.wait()


def border(centre, done, last_l, last_r, weights, bias):
    th, tw, c = done.shape
    vmem, hbm = pl.BlockSpec(memory_space=pltpu.VMEM), pl.BlockSpec(memory_space=pltpu.HBM)
    return pl.pallas_call(
        border_kernel,
        out_shape=jax.ShapeDtypeStruct((th, tw, c), BF16),
        in_specs=[vmem] * 6,
        out_specs=hbm,
        scratch_shapes=[pltpu.VMEM((SPAN, tw, c), BF16), pltpu.SemaphoreType.DMA((3,))],
        compiler_params=pltpu.CompilerParams(vmem_limit_bytes=24 * 2**20),
        cost_estimate=pl.CostEstimate(
            flops=2 * 6 * SPAN * tw * c * c, bytes_accessed=2 * th * tw * c, transcendentals=SPAN * tw * c
        ),
        name="border",
    )(centre, done, last_l, last_r, weights, bias)


def solution(mesh):
    rows, cols = mesh.shape["row"], mesh.shape["col"]

    def on_device(image, proj_in, taps_wide, taps_tall, proj_out, bias):
        bias = bias[None, :]
        held = [pltpu.with_memory_space_constraint(x, pltpu.HBM) for x in (image, proj_in, taps_wide, taps_tall, proj_out)]
        return border(*interior(rows, cols, *held, bias), bias)

    in_specs = (P("row", "col", None), P(), P(), P(), P(), P())
    out_specs = P("row", "col", None)
    return jax.shard_map(on_device, mesh=mesh, in_specs=in_specs, out_specs=out_specs, check_vma=False)
```

```python
import functools

import jax
import jax.numpy as jnp
from jax import lax
from jax.experimental import pallas as pl
from jax.experimental.pallas import tpu as pltpu
from jax.sharding import PartitionSpec as P

MESH = pl.DeviceIdType.MESH
F32, BF16 = jnp.float32, jnp.bfloat16
EDGE = 16
PAIRS = 3
SPAN = 2 * PAIRS
DEEP = SPAN + 2
PARTS = 4
BLOCK = 128
ROWS_OF = ((0, 2), (1, 2), (2, 1), (1, 3))


def interleave(*queues):
    pieces = [((i + 0.5) / len(queue), n, i) for n, queue in enumerate(queues) for i in range(len(queue))]
    for _, n, i in sorted(pieces):
        queues[n][i]()


def get_rows(ref, at):
    return jnp.concatenate([ref[n, at] for n in range(ref.shape[0])], 1)


def put_rows(ref, at, value):
    wide = ref.shape[2]
    for n in range(ref.shape[0]):
        ref[n, at] = value[:, n * wide : (n + 1) * wide]


def activated(t):
    return t + t * jnp.tanh(t)


def shifted(v, before, after):
    p = jnp.concatenate([v[1:], after], 0)
    return jnp.concatenate([before, v[:1], p[:-2]], 0), p


def product_pieces(pick, weights, half, total):
    c = weights.shape[2]
    state = {}

    def part(k, side):
        a, b = ROWS_OF[k]
        rows = [(pick(side, q, a), pick(side, q, b)) for q in range(PAIRS)]
        moved = jnp.concatenate([x + y if k == 1 else x - y for x, y in rows], 0)
        m = jnp.dot(moved, weights[k, side * c : (side + 1) * c], preferred_element_type=F32)
        state[k] = m if side == 0 else state[k] + m
        if side < 2:
            return
        if k == 2:
            m1 = state[1] + half[...]
            total[0] = m1 + state[2]
            total[1] = m1 - state[2]
        elif k == 0:
            total[0] = total[0] + state[0]
        elif k == 3:
            total[1] = total[1] - state[3]

    return [functools.partial(part, k, side) for two in ((1, 2), (0, 3)) for side in range(3) for k in two]


def interior_kernel(
    rows, cols,
    image, proj_in, taps_wide, taps_tall, proj_out, bias,
    done, top, bottom, halo_l, halo_r, corners, edge_l, edge_r, ends, before_l, before_r, kept, weights, half,
    centre, left_a, left_b, right_a, right_b, sum_a, sum_b, p_in, t_wide, t_tall, p_out, b_in,
    local_sem, stage_sem, send_sem, recv_sem,
):
    th, tw, c = image.shape
    steps = th // SPAN
    r, k = lax.axis_index("row"), lax.axis_index("col")
    up, down = lax.rem(r + rows - 1, rows), lax.rem(r + 1, rows)
    west, east = lax.rem(k + cols - 1, cols), lax.rem(k + 1, cols)
    above, below, before, behind = r > 0, r < rows - 1, k > 0, k < cols - 1
    around = [
        ((up, k), above), ((down, k), below), ((r, west), before), ((r, east), behind),
        ((up, west), above & before), ((down, east), below & behind), ((up, east), above & behind), ((down, west), below & before),
    ]

    barrier = pltpu.get_barrier_semaphore()
    for to, there in around:

        @pl.when(there)
        def _():
            pl.semaphore_signal(barrier, inc=1, device_id=to, device_id_type=MESH)

    def stage(s):
        return pltpu.make_async_copy(image.at[pl.ds(s * SPAN, SPAN)], centre.at[pl.ds(1 + s * SPAN, SPAN)], stage_sem.at[s])

    local = [
        pltpu.make_async_copy(src, dst, local_sem.at[i])
        for i, (src, dst) in enumerate(
            [(proj_in, p_in), (taps_wide, t_wide), (taps_tall, t_tall), (proj_out, p_out), (bias, b_in)]
        )
    ]
    for copy in local:
        copy.start()
    for s in range(steps):
        stage(s).start()

    zero = jnp.zeros((1, c), BF16)
    centre[0] = jnp.zeros((tw, c), BF16)
    centre[th + 1] = jnp.zeros((tw, c), BF16)

    def shift(at, left, right, i):
        left[i], right[i] = shifted(centre[at], zero, zero)

    for copy in local:
        copy.wait()
    half[...] = 0.5 * b_in[...]
    for s in range(2):
        stage(s).wait()

    base = p_in[...].astype(F32)
    g, split = {}, {}

    def scale(j, i):
        a = base * (0.25 * t_wide[pl.ds(j, 1)] * t_tall[pl.ds(i, 1)])
        high = a.astype(BF16)
        split[j, i] = high, (a - high.astype(F32)).astype(BF16)

    def weigh(j, i):
        high, low = split.pop((j, i))
        g[i] = jnp.dot(high, p_out[...], preferred_element_type=F32) + jnp.dot(low, p_out[...], preferred_element_type=F32)
        if i < 2:
            return
        at = pl.ds(j * c, c)
        ends = g[0] + g[2]
        weights[0, at] = (g[0] + g[0]).astype(BF16)
        weights[1, at] = (ends + g[1]).astype(BF16)
        weights[2, at] = (ends - g[1]).astype(BF16)
        weights[3, at] = (g[2] + g[2]).astype(BF16)

    taps = [(j, i) for j in range(3) for i in range(3)]
    scale(*taps[0])
    making = []
    for n, tap in enumerate(taps):
        if n + 1 < len(taps):
            making.append(functools.partial(scale, *taps[n + 1]))
        making.append(functools.partial(weigh, *tap))
    interleave(making, [functools.partial(shift, i, left_a, right_a, i) for i in range(DEEP)])

    def multiply(s, left, right, total):
        def pick(side, q, i):
            if side == 1:
                return centre[SPAN * s + 2 * q + i]
            return (left, None, right)[side][2 * q + i]

        return product_pieces(pick, weights, half, total)

    def finish(s, total, slots):
        def part(q, i, n):
            row = SPAN * s + 2 * q + i
            pair = pl.ds(PAIRS * s + q, 1)
            across = pl.ds(n * BLOCK, BLOCK)
            t = total[i, pl.ds(q * tw + n * BLOCK, BLOCK)]
            done[row, across] = (centre[row + 1, across].astype(F32) + activated(t)).astype(BF16)
            if n == 0:
                before_l[i, pair] = t[:1]
            if n == tw // BLOCK - 1:
                before_r[i, pair] = t[BLOCK - 1 :]
            if (q, i) == (0, 0) and slots[0] is not None:
                kept[slots[0], across] = t
            if (q, i) == (PAIRS - 1, 1) and slots[1] is not None:
                kept[slots[1], across] = t

        return [functools.partial(part, q, i, n) for i in range(2) for q in range(PAIRS) for n in range(tw // BLOCK)]

    def prepare(s, left, right, old_left, old_right):
        def again(i):
            left[i] = old_left[SPAN + i]
            right[i] = old_right[SPAN + i]

        return [functools.partial(again, i) for i in range(2)] + [
            functools.partial(shift, SPAN * s + i, left, right, i) for i in range(2, DEEP)
        ]

    stage(2).wait()
    interleave(multiply(0, left_a, right_a, sum_a), prepare(1, left_b, right_b, left_a, right_a))
    for s in range(3, steps):
        stage(s).wait()

    ends[0] = centre[1]
    ends[1] = centre[th]
    edge_l[...] = centre[pl.ds(1, th), pl.ds(0, EDGE)][:, 0]
    edge_r[...] = centre[pl.ds(1, th), pl.ds(tw - EDGE, EDGE)][:, EDGE - 1]
    pl.semaphore_wait(barrier, sum(there.astype(jnp.int32) for _, there in around))

    first, last = pl.ds(0, EDGE), pl.ds(th - EDGE, EDGE)
    moves = [
        (centre.at[1], bottom),
        (centre.at[th], top),
        (edge_l, halo_r),
        (edge_r, halo_l),
        (edge_l.at[first], corners.at[0]),
        (edge_r.at[last], corners.at[3]),
        (edge_r.at[first], corners.at[1]),
        (edge_l.at[last], corners.at[2]),
    ]
    copies = [
        pltpu.make_async_remote_copy(
            src_ref=src, dst_ref=dst, send_sem=send_sem.at[i], recv_sem=recv_sem.at[i], device_id=around[i][0], device_id_type=MESH
        )
        for i, (src, dst) in enumerate(moves)
    ]
    for copy, (_, there) in zip(copies, around):
        pl.when(there)(copy.start)

    def two(n, carry):
        s = 2 * n + 1
        interleave(
            multiply(s, left_b, right_b, sum_b),
            finish(s - 1, sum_a, (jnp.minimum(n, 1), None)),
            prepare(s + 1, left_a, right_a, left_b, right_b),
        )
        interleave(
            multiply(s + 1, left_a, right_a, sum_a),
            finish(s, sum_b, (None, None)),
            prepare(s + 2, left_b, right_b, left_a, right_a),
        )
        return carry

    lax.fori_loop(0, (steps - 2) // 2, two, 0)
    interleave(multiply(steps - 1, left_b, right_b, sum_b), finish(steps - 2, sum_a, (None, None)))
    interleave(finish(steps - 1, sum_b, (None, 2)))

    def clear(ref):
        ref[...] = jnp.zeros(ref.shape, ref.dtype)

    for i, (copy, (_, there)) in enumerate(zip(copies, around)):
        pl.when(there)(copy.wait_send)
        comes = around[i ^ 1][1]
        pl.when(comes)(copy.wait_recv)
        pl.when(jnp.logical_not(comes))(functools.partial(clear, moves[i][1]))


def interior(rows, cols, image, proj_in, taps_wide, taps_tall, proj_out, bias):
    th, tw, c = image.shape
    rank = proj_in.shape[1]
    pairs = -(-th // 32) * 16
    vmem, hbm = pl.BlockSpec(memory_space=pltpu.VMEM), pl.BlockSpec(memory_space=pltpu.HBM)
    shape = jax.ShapeDtypeStruct
    out_shape = (
        shape((th, tw, c), BF16),
        *[shape((tw, c), BF16)] * 2,
        *[shape((th, c), BF16)] * 2,
        shape((4, EDGE, c), BF16),
        *[shape((th, c), BF16)] * 2,
        shape((2, tw, c), BF16),
        *[shape((2, pairs, c), F32)] * 2,
        shape((3, tw, c), F32),
        shape((4, 3 * c, c), BF16),
        shape((1, c), F32),
    )
    return pl.pallas_call(
        functools.partial(interior_kernel, rows, cols),
        out_shape=out_shape,
        in_specs=[hbm] * 6,
        out_specs=(vmem,) * len(out_shape),
        scratch_shapes=[pltpu.VMEM((th + 2, tw, c), BF16)]
        + [pltpu.VMEM((DEEP, tw, c), BF16)] * 4
        + [pltpu.VMEM((2, PAIRS * tw, c), F32)] * 2
        + [
            pltpu.VMEM((c, rank), BF16),
            pltpu.VMEM((3, rank), F32),
            pltpu.VMEM((3, rank), F32),
            pltpu.VMEM((rank, c), BF16),
            pltpu.VMEM((1, c), F32),
            pltpu.SemaphoreType.DMA((5,)),
            pltpu.SemaphoreType.DMA((th // SPAN,)),
            pltpu.SemaphoreType.DMA((8,)),
            pltpu.SemaphoreType.DMA((8,)),
        ],
        compiler_params=pltpu.CompilerParams(collective_id=0, has_side_effects=True, vmem_limit_bytes=44 * 2**20),
        cost_estimate=pl.CostEstimate(
            flops=2 * 6 * th * tw * c * c, bytes_accessed=2 * th * tw * c, transcendentals=th * tw * c
        ),
        name="interior",
    )(image, proj_in, taps_wide, taps_tall, proj_out, bias)


def border_kernel(
    done, top, bottom, halo_l, halo_r, corners, edge_l, edge_r, ends, before_l, before_r, kept, weights, half,
    out,
    block, strip_l, strip_r, column, own, new_l, new_r, add_l, add_r, out_sem,
):
    th, tw, c = done.shape
    pairs = before_l.shape[1]
    inner_rows, inner_cols = pl.ds(1, th - 2), pl.ds(EDGE, tw - 2 * EDGE)
    low, high = pl.ds(0, EDGE), pl.ds(tw - EDGE, EDGE)
    bounds = [1 + (th - 2) * i // PARTS for i in range(PARTS + 1)]
    copies = []
    for i in range(PARTS):
        at = pl.ds(bounds[i], bounds[i + 1] - bounds[i])
        copies.append(pltpu.make_async_copy(done.at[at, inner_cols], out.at[at, inner_cols], out_sem.at[4 + i]))
    for copy in copies:
        copy.start()

    column[...] = jnp.zeros_like(column)
    own[...] = jnp.zeros_like(own)
    for halo, edge, before, new, add, at in (
        (halo_l, edge_l, before_l, new_l, add_l, 0),
        (halo_r, edge_r, before_r, new_r, add_r, 2 * c),
    ):
        put_rows(column, pl.ds(8, th), halo[...].astype(F32))
        put_rows(own, pl.ds(0, th), edge[...].astype(F32))
        d = [get_rows(column, pl.ds(7 + i, pairs, stride=2)) for i in range(4)]
        m = [
            jnp.dot(v.astype(BF16), weights[i, pl.ds(at, c)], preferred_element_type=F32)
            for i, v in enumerate([d[0] - d[2], d[1] + d[2], d[2] - d[1], d[1] - d[3]])
        ]
        for i, y in enumerate([m[0] + m[1] + m[2], m[1] - m[2] - m[3]]):
            lines = pl.ds(i, pairs, stride=2)
            put_rows(add, lines, y)
            put_rows(new, lines, get_rows(own, lines) + activated(before[i] + y))

    line = lax.broadcasted_iota(jnp.int32, (EDGE, c), 0)
    is_first, is_last = (line == 0).astype(F32).astype(BF16), (line == EDGE - 1).astype(F32).astype(BF16)
    not_first, not_last = 1 - is_first, 1 - is_last
    for h in range(1, th - 1):
        strip_l[h] = done[h, low] * not_first + get_rows(new_l, pl.ds(h, 1)).astype(BF16) * is_first
        strip_r[h] = done[h, high] * not_last + get_rows(new_r, pl.ds(h, 1)).astype(BF16) * is_last
    copies += [
        pltpu.make_async_copy(strip_l.at[inner_rows], out.at[inner_rows, low], out_sem.at[0]),
        pltpu.make_async_copy(strip_r.at[inner_rows], out.at[inner_rows, high], out_sem.at[1]),
    ]
    for copy in copies[PARTS:]:
        copy.start()

    across = lax.broadcasted_iota(jnp.int32, (tw, c), 0)
    own_rows = (0, th - 1)
    for i, (halo, weight, from_l, from_r, at, slot) in enumerate([
        (top, 0, 3, 2, EDGE - 1, 0),
        (bottom, 3, 1, 0, 0, 2),
    ]):
        row = own_rows[i]
        v = halo[...]
        left, right = shifted(v, corners[from_l][at : at + 1], corners[from_r][at : at + 1])
        t = kept[slot] + jnp.dot(jnp.concatenate([left, v, right], 1), weights[weight], preferred_element_type=F32)
        t = t + jnp.where(across == 0, get_rows(add_l, pl.ds(row, 1)), 0.0)
        t = t + jnp.where(across == tw - 1, get_rows(add_r, pl.ds(row, 1)), 0.0)
        block[i] = (ends[i].astype(F32) + activated(t)).astype(BF16)
        copy = pltpu.make_async_copy(block.at[i], out.at[row], out_sem.at[2 + i])
        copy.start()
        copies.append(copy)
    for copy in copies:
        copy.wait()


def border(done, *others):
    th, tw, c = done.shape
    pairs = -(-th // 32) * 16
    halves = c // 128
    vmem, hbm = pl.BlockSpec(memory_space=pltpu.VMEM), pl.BlockSpec(memory_space=pltpu.HBM)
    return pl.pallas_call(
        border_kernel,
        out_shape=jax.ShapeDtypeStruct((th, tw, c), BF16),
        in_specs=[vmem] * (1 + len(others)),
        out_specs=hbm,
        scratch_shapes=[pltpu.VMEM((2, tw, c), BF16)]
        + [pltpu.VMEM((th, EDGE, c), BF16)] * 2
        + [pltpu.VMEM((halves, 2 * pairs + 16, 128), F32)]
        + [pltpu.VMEM((halves, 2 * pairs, 128), F32)] * 5
        + [pltpu.SemaphoreType.DMA((4 + PARTS,))],
        compiler_params=pltpu.CompilerParams(vmem_limit_bytes=16 * 2**20),
        cost_estimate=pl.CostEstimate(
            flops=2 * 2 * 3 * tw * c * c, bytes_accessed=2 * th * tw * c, transcendentals=2 * tw * c
        ),
        name="border",
    )(done, *others)


def solution(mesh):
    rows, cols = mesh.shape["row"], mesh.shape["col"]

    def on_device(image, proj_in, taps_wide, taps_tall, proj_out, bias):
        given = (image, proj_in, taps_wide, taps_tall, proj_out, bias[None, :])
        return border(*interior(rows, cols, *[pltpu.with_memory_space_constraint(x, pltpu.HBM) for x in given]))

    in_specs = (P("row", "col", None), P(), P(), P(), P(), P())
    out_specs = P("row", "col", None)
    return jax.shard_map(on_device, mesh=mesh, in_specs=in_specs, out_specs=out_specs, check_vma=False)
```

```python
import functools

import jax
import jax.numpy as jnp
from jax import lax
from jax.experimental import pallas as pl
from jax.experimental.pallas import tpu as pltpu
from jax.sharding import PartitionSpec as P

MESH = pl.DeviceIdType.MESH
F32, BF16 = jnp.float32, jnp.bfloat16
EDGE = 16
PAIRS = 3
SPAN = 2 * PAIRS
DEEP = SPAN + 2
PARTS = 4
BLOCK = 128
ROWS_OF = ((0, 2), (1, 2), (2, 1), (1, 3))


def interleave(*queues):
    pieces = [((i + 0.5) / len(queue), n, i) for n, queue in enumerate(queues) for i in range(len(queue))]
    for _, n, i in sorted(pieces):
        queues[n][i]()


def get_rows(ref, at):
    return jnp.concatenate([ref[n, at] for n in range(ref.shape[0])], 1)


def put_rows(ref, at, value):
    wide = ref.shape[2]
    for n in range(ref.shape[0]):
        ref[n, at] = value[:, n * wide : (n + 1) * wide]


def activated(t):
    return t + t * jnp.tanh(t)


def shifted(v, before, after):
    p = jnp.concatenate([v[1:], after], 0)
    return jnp.concatenate([before, v[:1], p[:-2]], 0), p


def product_pieces(pick, weights, half, total):
    c = weights.shape[2]
    state = {}

    def part(k, side):
        a, b = ROWS_OF[k]
        rows = [(pick(side, q, a), pick(side, q, b)) for q in range(PAIRS)]
        moved = jnp.concatenate([x + y if k == 1 else x - y for x, y in rows], 0)
        m = jnp.dot(moved, weights[k, side * c : (side + 1) * c], preferred_element_type=F32)
        state[k] = m if side == 0 else state[k] + m
        if side < 2:
            return
        if k == 2:
            m1 = state[1] + half[...]
            total[0] = m1 + state[2]
            total[1] = m1 - state[2]
        elif k == 0:
            total[0] = total[0] + state[0]
        elif k == 3:
            total[1] = total[1] - state[3]

    return [functools.partial(part, k, side) for two in ((1, 2), (0, 3)) for side in range(3) for k in two]


def interior_kernel(
    rows, cols,
    image, proj_in, taps_wide, taps_tall, proj_out, bias,
    done, top, bottom, halo_l, halo_r, corners, edge_l, edge_r, ends, before_l, before_r, kept, weights, half,
    centre, left_a, left_b, right_a, right_b, sum_a, sum_b, p_in, t_wide, t_tall, p_out, b_in,
    local_sem, stage_sem, send_sem, recv_sem,
):
    th, tw, c = image.shape
    steps = th // SPAN
    r, k = lax.axis_index("row"), lax.axis_index("col")
    up, down = lax.rem(r + rows - 1, rows), lax.rem(r + 1, rows)
    west, east = lax.rem(k + cols - 1, cols), lax.rem(k + 1, cols)
    above, below, before, behind = r > 0, r < rows - 1, k > 0, k < cols - 1
    around = [
        ((up, k), above), ((down, k), below), ((r, west), before), ((r, east), behind),
        ((up, west), above & before), ((down, east), below & behind), ((up, east), above & behind), ((down, west), below & before),
    ]

    def stage(s):
        return pltpu.make_async_copy(image.at[pl.ds(s * SPAN, SPAN)], centre.at[pl.ds(1 + s * SPAN, SPAN)], stage_sem.at[s])

    local = [
        pltpu.make_async_copy(src, dst, local_sem.at[i])
        for i, (src, dst) in enumerate(
            [(proj_in, p_in), (taps_wide, t_wide), (taps_tall, t_tall), (proj_out, p_out), (bias, b_in)]
        )
    ]
    for copy in local:
        copy.start()
    for s in range(steps):
        stage(s).start()

    barrier = pltpu.get_barrier_semaphore()
    for to, there in around:

        @pl.when(there)
        def _():
            pl.semaphore_signal(barrier, inc=1, device_id=to, device_id_type=MESH)

    zero = jnp.zeros((1, c), BF16)
    centre[0] = jnp.zeros((tw, c), BF16)
    centre[th + 1] = jnp.zeros((tw, c), BF16)

    def shift(at, left, right, i):
        left[i], right[i] = shifted(centre[at], zero, zero)

    for copy in local:
        copy.wait()
    half[...] = 0.5 * b_in[...]
    for s in range(2):
        stage(s).wait()

    base = p_in[...].astype(F32)
    g, split = {}, {}

    def scale(j, i):
        a = base * (0.25 * t_wide[pl.ds(j, 1)] * t_tall[pl.ds(i, 1)])
        high = a.astype(BF16)
        split[j, i] = high, (a - high.astype(F32)).astype(BF16)

    def weigh(j, i):
        high, low = split.pop((j, i))
        g[i] = jnp.dot(high, p_out[...], preferred_element_type=F32) + jnp.dot(low, p_out[...], preferred_element_type=F32)
        if i < 2:
            return
        at = pl.ds(j * c, c)
        ends = g[0] + g[2]
        weights[0, at] = (g[0] + g[0]).astype(BF16)
        weights[1, at] = (ends + g[1]).astype(BF16)
        weights[2, at] = (ends - g[1]).astype(BF16)
        weights[3, at] = (g[2] + g[2]).astype(BF16)

    taps = [(j, i) for j in range(3) for i in range(3)]
    scale(*taps[0])
    making = []
    for n, tap in enumerate(taps):
        if n + 1 < len(taps):
            making.append(functools.partial(scale, *taps[n + 1]))
        making.append(functools.partial(weigh, *tap))
    interleave(making, [functools.partial(shift, i, left_a, right_a, i) for i in range(DEEP)])

    def multiply(s, left, right, total):
        def pick(side, q, i):
            if side == 1:
                return centre[SPAN * s + 2 * q + i]
            return (left, None, right)[side][2 * q + i]

        return product_pieces(pick, weights, half, total)

    def finish(s, total, slots):
        def part(q, i, n):
            row = SPAN * s + 2 * q + i
            pair = pl.ds(PAIRS * s + q, 1)
            across = pl.ds(n * BLOCK, BLOCK)
            t = total[i, pl.ds(q * tw + n * BLOCK, BLOCK)]
            done[row, across] = (centre[row + 1, across].astype(F32) + activated(t)).astype(BF16)
            if n == 0:
                before_l[i, pair] = t[:1]
            if n == tw // BLOCK - 1:
                before_r[i, pair] = t[BLOCK - 1 :]
            if (q, i) == (0, 0) and slots[0] is not None:
                kept[slots[0], across] = t
            if (q, i) == (PAIRS - 1, 1) and slots[1] is not None:
                kept[slots[1], across] = t

        return [functools.partial(part, q, i, n) for i in range(2) for q in range(PAIRS) for n in range(tw // BLOCK)]

    def prepare(s, left, right, old_left, old_right):
        def again(i):
            left[i] = old_left[SPAN + i]
            right[i] = old_right[SPAN + i]

        return [functools.partial(again, i) for i in range(2)] + [
            functools.partial(shift, SPAN * s + i, left, right, i) for i in range(2, DEEP)
        ]

    stage(2).wait()
    interleave(multiply(0, left_a, right_a, sum_a), prepare(1, left_b, right_b, left_a, right_a))
    for s in range(3, steps):
        stage(s).wait()

    ends[0] = centre[1]
    ends[1] = centre[th]
    edge_l[...] = centre[pl.ds(1, th), pl.ds(0, EDGE)][:, 0]
    edge_r[...] = centre[pl.ds(1, th), pl.ds(tw - EDGE, EDGE)][:, EDGE - 1]
    pl.semaphore_wait(barrier, sum(there.astype(jnp.int32) for _, there in around))

    first, last = pl.ds(0, EDGE), pl.ds(th - EDGE, EDGE)
    moves = [
        (centre.at[1], bottom),
        (centre.at[th], top),
        (edge_l, halo_r),
        (edge_r, halo_l),
        (edge_l.at[first], corners.at[0]),
        (edge_r.at[last], corners.at[3]),
        (edge_r.at[first], corners.at[1]),
        (edge_l.at[last], corners.at[2]),
    ]
    copies = [
        pltpu.make_async_remote_copy(
            src_ref=src, dst_ref=dst, send_sem=send_sem.at[i], recv_sem=recv_sem.at[i], device_id=around[i][0], device_id_type=MESH
        )
        for i, (src, dst) in enumerate(moves)
    ]
    for i in (4, 5, 6, 7, 2, 3, 0, 1):
        pl.when(around[i][1])(copies[i].start)

    def two(n, carry):
        s = 2 * n + 1
        interleave(
            multiply(s, left_b, right_b, sum_b),
            finish(s - 1, sum_a, (jnp.minimum(n, 1), None)),
            prepare(s + 1, left_a, right_a, left_b, right_b),
        )
        interleave(
            multiply(s + 1, left_a, right_a, sum_a),
            finish(s, sum_b, (None, None)),
            prepare(s + 2, left_b, right_b, left_a, right_a),
        )
        return carry

    lax.fori_loop(0, (steps - 2) // 2, two, 0)
    interleave(multiply(steps - 1, left_b, right_b, sum_b), finish(steps - 2, sum_a, (None, None)))
    interleave(finish(steps - 1, sum_b, (None, 2)))

    def clear(ref):
        ref[...] = jnp.zeros(ref.shape, ref.dtype)

    for i, (copy, (_, there)) in enumerate(zip(copies, around)):
        pl.when(there)(copy.wait_send)
        comes = around[i ^ 1][1]
        pl.when(comes)(copy.wait_recv)
        pl.when(jnp.logical_not(comes))(functools.partial(clear, moves[i][1]))


def interior(rows, cols, image, proj_in, taps_wide, taps_tall, proj_out, bias):
    th, tw, c = image.shape
    rank = proj_in.shape[1]
    pairs = -(-th // 32) * 16
    vmem, hbm = pl.BlockSpec(memory_space=pltpu.VMEM), pl.BlockSpec(memory_space=pltpu.HBM)
    shape = jax.ShapeDtypeStruct
    out_shape = (
        shape((th, tw, c), BF16),
        *[shape((tw, c), BF16)] * 2,
        *[shape((th, c), BF16)] * 2,
        shape((4, EDGE, c), BF16),
        *[shape((th, c), BF16)] * 2,
        shape((2, tw, c), BF16),
        *[shape((2, pairs, c), F32)] * 2,
        shape((3, tw, c), F32),
        shape((4, 3 * c, c), BF16),
        shape((1, c), F32),
    )
    return pl.pallas_call(
        functools.partial(interior_kernel, rows, cols),
        out_shape=out_shape,
        in_specs=[hbm] * 6,
        out_specs=(vmem,) * len(out_shape),
        scratch_shapes=[pltpu.VMEM((th + 2, tw, c), BF16)]
        + [pltpu.VMEM((DEEP, tw, c), BF16)] * 4
        + [pltpu.VMEM((2, PAIRS * tw, c), F32)] * 2
        + [
            pltpu.VMEM((c, rank), BF16),
            pltpu.VMEM((3, rank), F32),
            pltpu.VMEM((3, rank), F32),
            pltpu.VMEM((rank, c), BF16),
            pltpu.VMEM((1, c), F32),
            pltpu.SemaphoreType.DMA((5,)),
            pltpu.SemaphoreType.DMA((th // SPAN,)),
            pltpu.SemaphoreType.DMA((8,)),
            pltpu.SemaphoreType.DMA((8,)),
        ],
        compiler_params=pltpu.CompilerParams(collective_id=0, has_side_effects=True, vmem_limit_bytes=44 * 2**20),
        cost_estimate=pl.CostEstimate(
            flops=2 * 6 * th * tw * c * c, bytes_accessed=2 * th * tw * c, transcendentals=th * tw * c
        ),
        name="interior",
    )(image, proj_in, taps_wide, taps_tall, proj_out, bias)


def border_kernel(
    done, top, bottom, halo_l, halo_r, corners, edge_l, edge_r, ends, before_l, before_r, kept, weights, half,
    out,
    block, strip_l, strip_r, column, own, new_l, new_r, add_l, add_r, out_sem,
):
    th, tw, c = done.shape
    pairs = before_l.shape[1]
    inner_rows, inner_cols = pl.ds(1, th - 2), pl.ds(EDGE, tw - 2 * EDGE)
    low, high = pl.ds(0, EDGE), pl.ds(tw - EDGE, EDGE)
    bounds = [1 + (th - 2) * i // PARTS for i in range(PARTS + 1)]
    copies = []
    for i in range(PARTS):
        at = pl.ds(bounds[i], bounds[i + 1] - bounds[i])
        copies.append(pltpu.make_async_copy(done.at[at, inner_cols], out.at[at, inner_cols], out_sem.at[4 + i]))
    for copy in copies:
        copy.start()

    column[...] = jnp.zeros_like(column)
    own[...] = jnp.zeros_like(own)
    for halo, edge, before, new, add, at in (
        (halo_l, edge_l, before_l, new_l, add_l, 0),
        (halo_r, edge_r, before_r, new_r, add_r, 2 * c),
    ):
        put_rows(column, pl.ds(8, th), halo[...].astype(F32))
        put_rows(own, pl.ds(0, th), edge[...].astype(F32))
        d = [get_rows(column, pl.ds(7 + i, pairs, stride=2)) for i in range(4)]
        m = [
            jnp.dot(v.astype(BF16), weights[i, pl.ds(at, c)], preferred_element_type=F32)
            for i, v in enumerate([d[0] - d[2], d[1] + d[2], d[2] - d[1], d[1] - d[3]])
        ]
        for i, y in enumerate([m[0] + m[1] + m[2], m[1] - m[2] - m[3]]):
            lines = pl.ds(i, pairs, stride=2)
            put_rows(add, lines, y)
            put_rows(new, lines, get_rows(own, lines) + activated(before[i] + y))

    line = lax.broadcasted_iota(jnp.int32, (EDGE, c), 0)
    is_first, is_last = (line == 0).astype(F32).astype(BF16), (line == EDGE - 1).astype(F32).astype(BF16)
    not_first, not_last = 1 - is_first, 1 - is_last
    for h in range(1, th - 1):
        strip_l[h] = done[h, low] * not_first + get_rows(new_l, pl.ds(h, 1)).astype(BF16) * is_first
        strip_r[h] = done[h, high] * not_last + get_rows(new_r, pl.ds(h, 1)).astype(BF16) * is_last
    copies += [
        pltpu.make_async_copy(strip_l.at[inner_rows], out.at[inner_rows, low], out_sem.at[0]),
        pltpu.make_async_copy(strip_r.at[inner_rows], out.at[inner_rows, high], out_sem.at[1]),
    ]
    for copy in copies[PARTS:]:
        copy.start()

    across = lax.broadcasted_iota(jnp.int32, (tw, c), 0)
    own_rows = (0, th - 1)
    for i, (halo, weight, from_l, from_r, at, slot) in enumerate([
        (top, 0, 3, 2, EDGE - 1, 0),
        (bottom, 3, 1, 0, 0, 2),
    ]):
        row = own_rows[i]
        v = halo[...]
        left, right = shifted(v, corners[from_l][at : at + 1], corners[from_r][at : at + 1])
        t = kept[slot] + jnp.dot(jnp.concatenate([left, v, right], 1), weights[weight], preferred_element_type=F32)
        t = t + jnp.where(across == 0, get_rows(add_l, pl.ds(row, 1)), 0.0)
        t = t + jnp.where(across == tw - 1, get_rows(add_r, pl.ds(row, 1)), 0.0)
        block[i] = (ends[i].astype(F32) + activated(t)).astype(BF16)
        copy = pltpu.make_async_copy(block.at[i], out.at[row], out_sem.at[2 + i])
        copy.start()
        copies.append(copy)
    for copy in copies:
        copy.wait()


def border(done, *others):
    th, tw, c = done.shape
    pairs = -(-th // 32) * 16
    halves = c // 128
    vmem, hbm = pl.BlockSpec(memory_space=pltpu.VMEM), pl.BlockSpec(memory_space=pltpu.HBM)
    return pl.pallas_call(
        border_kernel,
        out_shape=jax.ShapeDtypeStruct((th, tw, c), BF16),
        in_specs=[vmem] * (1 + len(others)),
        out_specs=hbm,
        scratch_shapes=[pltpu.VMEM((2, tw, c), BF16)]
        + [pltpu.VMEM((th, EDGE, c), BF16)] * 2
        + [pltpu.VMEM((halves, 2 * pairs + 16, 128), F32)]
        + [pltpu.VMEM((halves, 2 * pairs, 128), F32)] * 5
        + [pltpu.SemaphoreType.DMA((4 + PARTS,))],
        compiler_params=pltpu.CompilerParams(vmem_limit_bytes=16 * 2**20),
        cost_estimate=pl.CostEstimate(
            flops=2 * 2 * 3 * tw * c * c, bytes_accessed=2 * th * tw * c, transcendentals=2 * tw * c
        ),
        name="border",
    )(done, *others)


def solution(mesh):
    rows, cols = mesh.shape["row"], mesh.shape["col"]

    def on_device(image, proj_in, taps_wide, taps_tall, proj_out, bias):
        given = (image, proj_in, taps_wide, taps_tall, proj_out, bias[None, :])
        return border(*interior(rows, cols, *[pltpu.with_memory_space_constraint(x, pltpu.HBM) for x in given]))

    in_specs = (P("row", "col", None), P(), P(), P(), P(), P())
    out_specs = P("row", "col", None)
    return jax.shard_map(on_device, mesh=mesh, in_specs=in_specs, out_specs=out_specs, check_vma=False)
```

```python
import functools

import jax
import jax.numpy as jnp
from jax import lax
from jax.experimental import pallas as pl
from jax.experimental.pallas import tpu as pltpu
from jax.sharding import PartitionSpec as P

MESH = pl.DeviceIdType.MESH
F32, BF16 = jnp.float32, jnp.bfloat16
EDGE = 16
PAIRS = 3
SPAN = 2 * PAIRS
DEEP = SPAN + 2
PARTS = 4
BLOCK = 128
ROWS_OF = ((0, 2), (1, 2), (2, 1), (1, 3))


def interleave(*queues):
    pieces = [((i + 0.5) / len(queue), n, i) for n, queue in enumerate(queues) for i in range(len(queue))]
    for _, n, i in sorted(pieces):
        queues[n][i]()


def get_rows(ref, at):
    return jnp.concatenate([ref[n, at] for n in range(ref.shape[0])], 1)


def put_rows(ref, at, value):
    wide = ref.shape[2]
    for n in range(ref.shape[0]):
        ref[n, at] = value[:, n * wide : (n + 1) * wide]


def activated(t):
    return t + t * jnp.tanh(t)


def shifted(v, before, after):
    p = jnp.concatenate([v[1:], after], 0)
    return jnp.concatenate([before, v[:1], p[:-2]], 0), p


def product_pieces(pick, weights, half, total):
    c = weights.shape[2]
    state = {}

    def part(k, side):
        a, b = ROWS_OF[k]
        rows = [(pick(side, q, a), pick(side, q, b)) for q in range(PAIRS)]
        moved = jnp.concatenate([x + y if k == 1 else x - y for x, y in rows], 0)
        m = jnp.dot(moved, weights[k, side * c : (side + 1) * c], preferred_element_type=F32)
        state[k] = m if side == 0 else state[k] + m
        if side < 2:
            return
        if k == 2:
            m1 = state[1] + half[...]
            total[0] = m1 + state[2]
            total[1] = m1 - state[2]
        elif k == 0:
            total[0] = total[0] + state[0]
        elif k == 3:
            total[1] = total[1] - state[3]

    return [functools.partial(part, k, side) for two in ((1, 2), (0, 3)) for side in range(3) for k in two]


def interior_kernel(
    rows, cols,
    image, proj_in, taps_wide, taps_tall, proj_out, bias,
    done, top, bottom, halo_l, halo_r, corners, edge_l, edge_r, ends, before_l, before_r, kept, weights, half,
    centre, left_a, left_b, right_a, right_b, sum_a, sum_b, p_in, t_wide, t_tall, p_out, b_in,
    local_sem, stage_sem, send_sem, recv_sem,
):
    th, tw, c = image.shape
    steps = th // SPAN
    r, k = lax.axis_index("row"), lax.axis_index("col")
    up, down = lax.rem(r + rows - 1, rows), lax.rem(r + 1, rows)
    west, east = lax.rem(k + cols - 1, cols), lax.rem(k + 1, cols)
    above, below, before, behind = r > 0, r < rows - 1, k > 0, k < cols - 1
    around = [
        ((up, k), above), ((down, k), below), ((r, west), before), ((r, east), behind),
        ((up, west), above & before), ((down, east), below & behind), ((up, east), above & behind), ((down, west), below & before),
    ]

    def stage(s):
        return pltpu.make_async_copy(image.at[pl.ds(s * SPAN, SPAN)], centre.at[pl.ds(1 + s * SPAN, SPAN)], stage_sem.at[s])

    local = [
        pltpu.make_async_copy(src, dst, local_sem.at[i])
        for i, (src, dst) in enumerate(
            [(proj_in, p_in), (taps_wide, t_wide), (taps_tall, t_tall), (proj_out, p_out), (bias, b_in)]
        )
    ]
    for copy in local:
        copy.start()
    for s in range(steps):
        stage(s).start()

    barrier = pltpu.get_barrier_semaphore()
    for to, there in around:

        @pl.when(there)
        def _():
            pl.semaphore_signal(barrier, inc=1, device_id=to, device_id_type=MESH)

    zero = jnp.zeros((1, c), BF16)
    centre[0] = jnp.zeros((tw, c), BF16)
    centre[th + 1] = jnp.zeros((tw, c), BF16)

    def shift(at, left, right, i):
        left[i], right[i] = shifted(centre[at], zero, zero)

    for copy in local:
        copy.wait()
    half[...] = 0.5 * b_in[...]

    base = p_in[...].astype(F32)
    g, split = {}, {}

    def scale(j, i):
        a = base * (0.25 * t_wide[pl.ds(j, 1)] * t_tall[pl.ds(i, 1)])
        high = a.astype(BF16)
        split[j, i] = high, (a - high.astype(F32)).astype(BF16)

    def weigh(j, i):
        high, low = split.pop((j, i))
        g[i] = jnp.dot(high, p_out[...], preferred_element_type=F32) + jnp.dot(low, p_out[...], preferred_element_type=F32)
        if i < 2:
            return
        at = pl.ds(j * c, c)
        ends = g[0] + g[2]
        weights[0, at] = (g[0] + g[0]).astype(BF16)
        weights[1, at] = (ends + g[1]).astype(BF16)
        weights[2, at] = (ends - g[1]).astype(BF16)
        weights[3, at] = (g[2] + g[2]).astype(BF16)

    taps = [(j, i) for j in range(3) for i in range(3)]
    scale(*taps[0])
    making = []
    for n, tap in enumerate(taps):
        if n + 1 < len(taps):
            making.append(functools.partial(scale, *taps[n + 1]))
        making.append(functools.partial(weigh, *tap))
    ahead = len(making) // 3
    interleave(making[:ahead])
    for s in range(2):
        stage(s).wait()
    interleave(making[ahead:], [functools.partial(shift, i, left_a, right_a, i) for i in range(DEEP)])

    def multiply(s, left, right, total):
        def pick(side, q, i):
            if side == 1:
                return centre[SPAN * s + 2 * q + i]
            return (left, None, right)[side][2 * q + i]

        return product_pieces(pick, weights, half, total)

    def finish(s, total, slots):
        def part(q, i, n):
            row = SPAN * s + 2 * q + i
            pair = pl.ds(PAIRS * s + q, 1)
            across = pl.ds(n * BLOCK, BLOCK)
            t = total[i, pl.ds(q * tw + n * BLOCK, BLOCK)]
            done[row, across] = (centre[row + 1, across].astype(F32) + activated(t)).astype(BF16)
            if n == 0:
                before_l[i, pair] = t[:1]
            if n == tw // BLOCK - 1:
                before_r[i, pair] = t[BLOCK - 1 :]
            if (q, i) == (0, 0) and slots[0] is not None:
                kept[slots[0], across] = t
            if (q, i) == (PAIRS - 1, 1) and slots[1] is not None:
                kept[slots[1], across] = t

        return [functools.partial(part, q, i, n) for i in range(2) for q in range(PAIRS) for n in range(tw // BLOCK)]

    def prepare(s, left, right, old_left, old_right):
        def again(i):
            left[i] = old_left[SPAN + i]
            right[i] = old_right[SPAN + i]

        return [functools.partial(again, i) for i in range(2)] + [
            functools.partial(shift, SPAN * s + i, left, right, i) for i in range(2, DEEP)
        ]

    stage(2).wait()
    interleave(multiply(0, left_a, right_a, sum_a), prepare(1, left_b, right_b, left_a, right_a))
    for s in range(3, steps):
        stage(s).wait()

    ends[0] = centre[1]
    ends[1] = centre[th]
    edge_l[...] = centre[pl.ds(1, th), pl.ds(0, EDGE)][:, 0]
    edge_r[...] = centre[pl.ds(1, th), pl.ds(tw - EDGE, EDGE)][:, EDGE - 1]
    pl.semaphore_wait(barrier, sum(there.astype(jnp.int32) for _, there in around))

    first, last = pl.ds(0, EDGE), pl.ds(th - EDGE, EDGE)
    moves = [
        (centre.at[1], bottom),
        (centre.at[th], top),
        (edge_l, halo_r),
        (edge_r, halo_l),
        (edge_l.at[first], corners.at[0]),
        (edge_r.at[last], corners.at[3]),
        (edge_r.at[first], corners.at[1]),
        (edge_l.at[last], corners.at[2]),
    ]
    copies = [
        pltpu.make_async_remote_copy(
            src_ref=src, dst_ref=dst, send_sem=send_sem.at[i], recv_sem=recv_sem.at[i], device_id=around[i][0], device_id_type=MESH
        )
        for i, (src, dst) in enumerate(moves)
    ]
    for i in (4, 5, 6, 7, 2, 3, 0, 1):
        pl.when(around[i][1])(copies[i].start)

    def two(n, carry):
        s = 2 * n + 1
        interleave(
            multiply(s, left_b, right_b, sum_b),
            finish(s - 1, sum_a, (jnp.minimum(n, 1), None)),
            prepare(s + 1, left_a, right_a, left_b, right_b),
        )
        interleave(
            multiply(s + 1, left_a, right_a, sum_a),
            finish(s, sum_b, (None, None)),
            prepare(s + 2, left_b, right_b, left_a, right_a),
        )
        return carry

    lax.fori_loop(0, (steps - 2) // 2, two, 0)
    interleave(multiply(steps - 1, left_b, right_b, sum_b), finish(steps - 2, sum_a, (None, None)))
    interleave(finish(steps - 1, sum_b, (None, 2)))

    def clear(ref):
        ref[...] = jnp.zeros(ref.shape, ref.dtype)

    for i, (copy, (_, there)) in enumerate(zip(copies, around)):
        pl.when(there)(copy.wait_send)
        comes = around[i ^ 1][1]
        pl.when(comes)(copy.wait_recv)
        pl.when(jnp.logical_not(comes))(functools.partial(clear, moves[i][1]))


def interior(rows, cols, image, proj_in, taps_wide, taps_tall, proj_out, bias):
    th, tw, c = image.shape
    rank = proj_in.shape[1]
    pairs = -(-th // 32) * 16
    vmem, hbm = pl.BlockSpec(memory_space=pltpu.VMEM), pl.BlockSpec(memory_space=pltpu.HBM)
    shape = jax.ShapeDtypeStruct
    out_shape = (
        shape((th, tw, c), BF16),
        *[shape((tw, c), BF16)] * 2,
        *[shape((th, c), BF16)] * 2,
        shape((4, EDGE, c), BF16),
        *[shape((th, c), BF16)] * 2,
        shape((2, tw, c), BF16),
        *[shape((2, pairs, c), F32)] * 2,
        shape((3, tw, c), F32),
        shape((4, 3 * c, c), BF16),
        shape((1, c), F32),
    )
    return pl.pallas_call(
        functools.partial(interior_kernel, rows, cols),
        out_shape=out_shape,
        in_specs=[hbm] * 6,
        out_specs=(vmem,) * len(out_shape),
        scratch_shapes=[pltpu.VMEM((th + 2, tw, c), BF16)]
        + [pltpu.VMEM((DEEP, tw, c), BF16)] * 4
        + [pltpu.VMEM((2, PAIRS * tw, c), F32)] * 2
        + [
            pltpu.VMEM((c, rank), BF16),
            pltpu.VMEM((3, rank), F32),
            pltpu.VMEM((3, rank), F32),
            pltpu.VMEM((rank, c), BF16),
            pltpu.VMEM((1, c), F32),
            pltpu.SemaphoreType.DMA((5,)),
            pltpu.SemaphoreType.DMA((th // SPAN,)),
            pltpu.SemaphoreType.DMA((8,)),
            pltpu.SemaphoreType.DMA((8,)),
        ],
        compiler_params=pltpu.CompilerParams(collective_id=0, has_side_effects=True, vmem_limit_bytes=44 * 2**20),
        cost_estimate=pl.CostEstimate(
            flops=2 * 6 * th * tw * c * c, bytes_accessed=2 * th * tw * c, transcendentals=th * tw * c
        ),
        name="interior",
    )(image, proj_in, taps_wide, taps_tall, proj_out, bias)


def border_kernel(
    done, top, bottom, halo_l, halo_r, corners, edge_l, edge_r, ends, before_l, before_r, kept, weights, half,
    out,
    block, strip_l, strip_r, column, own, new_l, new_r, add_l, add_r, out_sem,
):
    th, tw, c = done.shape
    pairs = before_l.shape[1]
    inner_rows, inner_cols = pl.ds(1, th - 2), pl.ds(EDGE, tw - 2 * EDGE)
    low, high = pl.ds(0, EDGE), pl.ds(tw - EDGE, EDGE)
    bounds = [1 + (th - 2) * i // PARTS for i in range(PARTS + 1)]
    copies = []
    for i in range(PARTS):
        at = pl.ds(bounds[i], bounds[i + 1] - bounds[i])
        copies.append(pltpu.make_async_copy(done.at[at, inner_cols], out.at[at, inner_cols], out_sem.at[4 + i]))
    for copy in copies:
        copy.start()

    column[...] = jnp.zeros_like(column)
    own[...] = jnp.zeros_like(own)
    for halo, edge, before, new, add, at in (
        (halo_l, edge_l, before_l, new_l, add_l, 0),
        (halo_r, edge_r, before_r, new_r, add_r, 2 * c),
    ):
        put_rows(column, pl.ds(8, th), halo[...].astype(F32))
        put_rows(own, pl.ds(0, th), edge[...].astype(F32))
        d = [get_rows(column, pl.ds(7 + i, pairs, stride=2)) for i in range(4)]
        m = [
            jnp.dot(v.astype(BF16), weights[i, pl.ds(at, c)], preferred_element_type=F32)
            for i, v in enumerate([d[0] - d[2], d[1] + d[2], d[2] - d[1], d[1] - d[3]])
        ]
        for i, y in enumerate([m[0] + m[1] + m[2], m[1] - m[2] - m[3]]):
            lines = pl.ds(i, pairs, stride=2)
            put_rows(add, lines, y)
            put_rows(new, lines, get_rows(own, lines) + activated(before[i] + y))

    line = lax.broadcasted_iota(jnp.int32, (EDGE, c), 0)
    is_first, is_last = (line == 0).astype(F32).astype(BF16), (line == EDGE - 1).astype(F32).astype(BF16)
    not_first, not_last = 1 - is_first, 1 - is_last
    for h in range(1, th - 1):
        strip_l[h] = done[h, low] * not_first + get_rows(new_l, pl.ds(h, 1)).astype(BF16) * is_first
        strip_r[h] = done[h, high] * not_last + get_rows(new_r, pl.ds(h, 1)).astype(BF16) * is_last
    copies += [
        pltpu.make_async_copy(strip_l.at[inner_rows], out.at[inner_rows, low], out_sem.at[0]),
        pltpu.make_async_copy(strip_r.at[inner_rows], out.at[inner_rows, high], out_sem.at[1]),
    ]
    for copy in copies[PARTS:]:
        copy.start()

    across = lax.broadcasted_iota(jnp.int32, (tw, c), 0)
    own_rows = (0, th - 1)
    for i, (halo, weight, from_l, from_r, at, slot) in enumerate([
        (top, 0, 3, 2, EDGE - 1, 0),
        (bottom, 3, 1, 0, 0, 2),
    ]):
        row = own_rows[i]
        v = halo[...]
        left, right = shifted(v, corners[from_l][at : at + 1], corners[from_r][at : at + 1])
        t = kept[slot] + jnp.dot(jnp.concatenate([left, v, right], 1), weights[weight], preferred_element_type=F32)
        t = t + jnp.where(across == 0, get_rows(add_l, pl.ds(row, 1)), 0.0)
        t = t + jnp.where(across == tw - 1, get_rows(add_r, pl.ds(row, 1)), 0.0)
        block[i] = (ends[i].astype(F32) + activated(t)).astype(BF16)
        copy = pltpu.make_async_copy(block.at[i], out.at[row], out_sem.at[2 + i])
        copy.start()
        copies.append(copy)
    for copy in copies:
        copy.wait()


def border(done, *others):
    th, tw, c = done.shape
    pairs = -(-th // 32) * 16
    halves = c // 128
    vmem, hbm = pl.BlockSpec(memory_space=pltpu.VMEM), pl.BlockSpec(memory_space=pltpu.HBM)
    return pl.pallas_call(
        border_kernel,
        out_shape=jax.ShapeDtypeStruct((th, tw, c), BF16),
        in_specs=[vmem] * (1 + len(others)),
        out_specs=hbm,
        scratch_shapes=[pltpu.VMEM((2, tw, c), BF16)]
        + [pltpu.VMEM((th, EDGE, c), BF16)] * 2
        + [pltpu.VMEM((halves, 2 * pairs + 16, 128), F32)]
        + [pltpu.VMEM((halves, 2 * pairs, 128), F32)] * 5
        + [pltpu.SemaphoreType.DMA((4 + PARTS,))],
        compiler_params=pltpu.CompilerParams(vmem_limit_bytes=16 * 2**20),
        cost_estimate=pl.CostEstimate(
            flops=2 * 2 * 3 * tw * c * c, bytes_accessed=2 * th * tw * c, transcendentals=2 * tw * c
        ),
        name="border",
    )(done, *others)


def solution(mesh):
    rows, cols = mesh.shape["row"], mesh.shape["col"]

    def on_device(image, proj_in, taps_wide, taps_tall, proj_out, bias):
        given = (image, proj_in, taps_wide, taps_tall, proj_out, bias[None, :])
        return border(*interior(rows, cols, *[pltpu.with_memory_space_constraint(x, pltpu.HBM) for x in given]))

    in_specs = (P("row", "col", None), P(), P(), P(), P(), P())
    out_specs = P("row", "col", None)
    return jax.shard_map(on_device, mesh=mesh, in_specs=in_specs, out_specs=out_specs, check_vma=False)
```
